256 devices in a mesh: blk: 16 (over z_hi, y, core), rows: 16 (over x, z_lo).
Axes of the slice: x: 4, y: 4, z: 8 (z_hi: 2, z_lo: 4; z = z_hi * 4 + z_lo), core: 2. Of those that a mesh axis runs over, the one named last changes fastest.
Arguments:
- section_weights: bfloat16 [16, 256, 9, 256], P('blk'), may hold values from -0.125 to 0.125
- grad_acc: bfloat16 [16, 256, 9, 256], P('blk', 'rows'), may hold values from -6 to 6
- saved_inputs: bfloat16 [3, 16, 64, 256, 256], P(None, 'blk', 'rows'), may hold values from -6 to 6
- cotangent: bfloat16 [16, 64, 256, 256], P('blk', 'rows'), may hold values from -6 to 6
- fresh_grads: bfloat16 [2, 64, 256, 256], P(None, 'rows'), may hold values from -6 to 6
Outputs:
- tick_states: bfloat16 [3, 16, 64, 256, 256], P(None, 'blk', 'rows')
- grad_out: bfloat16 [16, 256, 9, 256], P('blk', 'rows')
The draws below stay inside these ranges and needn't reach their ends.
All inputs are finite; a program needn't handle non-finite values.
Results may differ from the reference program's by a relative error of at most 0.0057.
Values may be sent and summed in bfloat16 or wider, within the bound.
No kernel may reach another device: no remote copies, remote signals or barrier semaphores. Data moves between devices by JAX's collectives and lax.ppermute only.
A program may use at most 128 MiB of HBM per device.

```python
import jax
import jax.numpy as jnp
from jax import lax

CH = 256
TICKS = 3
COLS = 256
LAYERS = 16
IMAGES = 16
HEIGHT = 64


def block_levels(own_key, extent, pieces, smallest, high):
    gain, own = 1.0, jax.random.fold_in(own_key, 6)
    for axis_at, shards_of in pieces:
        draws = jnp.exp(jax.random.uniform(jax.random.fold_in(own, axis_at), (shards_of,), jnp.float32, smallest / len(pieces), high / len(pieces)))
        gain = gain * jnp.repeat(draws, extent[axis_at] // shards_of).reshape([-1 if axis == axis_at else 1 for axis in range(len(extent))])
    return gain


def normal_values(rng, shape, deviation, reach, cuts=(), kind=jnp.bfloat16):
    factor_of = block_levels(rng, shape, cuts, -0.22, 0.18) if cuts else 1.0
    values = jax.random.normal(rng, shape, jnp.float32) * deviation * factor_of
    return jnp.minimum(jnp.maximum(values, -reach), reach).astype(kind)


def setup_inputs(seed: int = 0) -> dict:
    keys = jax.random.split(jax.random.key(seed), 6)
    section_weights = normal_values(keys[0], (LAYERS, CH, 9, CH), (9 * CH) ** -0.5, 0.125, ((0, 16),))
    grad_acc = normal_values(keys[1], (LAYERS, CH, 9, CH), 1.0, 6.0, ((0, 16), (1, 16)))
    saved_inputs = normal_values(keys[2], (TICKS, IMAGES, HEIGHT, CH, COLS), 1.0, 6.0, ((1, 16), (2, 16)))
    cotangent = normal_values(keys[3], (IMAGES, HEIGHT, CH, COLS), 1.0, 6.0, ((0, 16), (1, 16)))
    fresh_grads = normal_values(keys[4], (TICKS - 1, HEIGHT, CH, COLS), 1.0, 6.0, ((1, 16),))
    return {"section_weights": section_weights, "grad_acc": grad_acc, "saved_inputs": saved_inputs, "cotangent": cotangent, "fresh_grads": fresh_grads}


def image_step(members):
    grad_now, saved_now, kernel = members
    height = grad_now.shape[0]
    columns = grad_now.shape[2]
    cell_scale = (saved_inputs_cells(height, columns)) ** -0.5
    inputs = jnp.maximum(saved_now, 0).astype(jnp.bfloat16)
    grad_float = grad_now.astype(jnp.float32)
    grad_wide = jnp.pad(grad_float, ((1, 1), (0, 0), (1, 1)))
    input_wide = jnp.pad(inputs.astype(jnp.float32), ((1, 1), (0, 0), (1, 1)))
    kernel_wide = kernel.astype(jnp.float32)
    back_sum = jnp.zeros(grad_now.shape, jnp.float32)
    tap_list = []
    for tap_index in range(9):
        row_shift = tap_index // 3
        col_shift = tap_index % 3
        window = grad_wide[2 - row_shift:2 - row_shift + height, :, 2 - col_shift:2 - col_shift + columns]
        back_sum = back_sum + jnp.einsum("oi,row->riw", kernel_wide[:, tap_index, :], window)
        source = input_wide[row_shift:row_shift + height, :, col_shift:col_shift + columns]
        tap_list.append(jnp.einsum("row,riw->oi", grad_float, source) * cell_scale)
    new_grads = jnp.where(saved_now > 0, back_sum, 0.0).astype(jnp.bfloat16)
    return new_grads, jnp.stack(tap_list, axis=1)


def saved_inputs_cells(height, columns):
    return float(height * columns)


def reference(section_weights, grad_acc, saved_inputs, cotangent, fresh_grads):
    images = cotangent.shape[0]
    current = cotangent
    running = grad_acc
    outputs = []
    for tick_index in range(TICKS):
        if tick_index > 0:
            restart = jnp.arange(images) == (images - tick_index) % images
            current = jnp.where(restart[:, None, None, None], fresh_grads[tick_index - 1][None], current)
        kernels = jnp.roll(section_weights, -tick_index, axis=0)
        new_grads, weight_grads = lax.map(image_step, (current, saved_inputs[tick_index], kernels))
        running = (running.astype(jnp.float32) + jnp.roll(weight_grads, tick_index, axis=0)).astype(jnp.bfloat16)
        outputs.append(new_grads)
        current = new_grads
    return jnp.stack(outputs), jnp.roll(running, -(TICKS - 1), axis=0)
```

```python
import functools

import jax
import jax.numpy as jnp
from jax import lax
from jax.experimental import pallas as pl
from jax.experimental.pallas import tpu as pltpu
from jax.sharding import PartitionSpec as P

TICKS = 3
BF = jnp.bfloat16
F32 = jnp.float32
VMEM_BYTES = 28 * 1024 * 1024


def whole(memory=pltpu.VMEM):
    return pl.BlockSpec(memory_space=memory)


def fill_shifted(shift_ref, rows):
    for index, row in enumerate(rows):
        wide = row.astype(F32)
        columns = wide.shape[1]
        place = lax.broadcasted_iota(jnp.int32, wide.shape, 1)
        ahead = pltpu.roll(wide, columns - 1, 1)
        behind = pltpu.roll(wide, 1, 1)
        shift_ref[0, index] = jnp.where(place == columns - 1, 0.0, ahead).astype(BF)
        shift_ref[1, index] = row
        shift_ref[2, index] = jnp.where(place == 0, 0.0, behind).astype(BF)


def back_kernel(tick, height, last, *refs):
    refs = list(refs)
    flag = None if last else refs.pop(0)
    up, top, mid, bot, down, kernel, saved = refs[:7]
    refs = refs[7:]
    fresh = None if last else refs.pop(0)
    if tick > 0:
        refs.pop(0)
    states = refs.pop(0)
    if not last:
        next_top, next_mid, next_bot = refs[:3]
        refs = refs[3:]
    shift_ref, turned, result, sem = refs
    channels = top.shape[0]
    rows = [up[...], top[...], *[mid[i] for i in range(height - 2)], bot[...], down[...]]
    fill_shifted(shift_ref, rows)
    for b in range(3):
        for j in range(3):
            turned[b, :, j * channels : (j + 1) * channels] = kernel[3 * (2 - j) + b].T
    for r in range(height):
        total = None
        for b in range(3):
            window = shift_ref[b, r : r + 3].reshape(3 * channels, -1)
            part = jnp.dot(turned[b], window, preferred_element_type=F32)
            total = part if total is None else total + part
        value = jnp.where(saved[r] > 0, total, 0.0).astype(BF)
        result[r] = value
        if not last:
            value = jnp.where(flag[0] > 0, fresh[r], value)
            if r == 0:
                next_top[...] = value
            elif r == height - 1:
                next_bot[...] = value
            else:
                next_mid[r - 1] = value
    copy = pltpu.make_async_copy(result, states.at[tick, 0], sem)
    copy.start()
    copy.wait()


def back_project(tick, edges, kernel, saved, states, restart, fresh):
    up, top, mid, bot, down = edges
    last = restart is None
    height, channels, columns = saved.shape
    args = ([] if last else [restart]) + [up, top, mid, bot, down, kernel, saved]
    specs = ([] if last else [whole(pltpu.SMEM)]) + [whole()] * 7
    if not last:
        args.append(fresh)
        specs.append(whole())
    alias = {}
    if tick > 0:
        alias = {len(args): 0}
        args.append(states)
        specs.append(whole(pl.ANY))
    shapes = [jax.ShapeDtypeStruct((TICKS, 1, height, channels, columns), BF)]
    if not last:
        shapes += [
            jax.ShapeDtypeStruct((channels, columns), BF),
            jax.ShapeDtypeStruct((height - 2, channels, columns), BF),
            jax.ShapeDtypeStruct((channels, columns), BF),
        ]
    return pl.pallas_call(
        functools.partial(back_kernel, tick, height, last),
        out_shape=shapes,
        in_specs=specs,
        out_specs=[whole(pl.ANY)] + [whole()] * (len(shapes) - 1),
        scratch_shapes=[
            pltpu.VMEM((3, height + 2, channels, columns), BF),
            pltpu.VMEM((3, channels, 3 * channels), BF),
            pltpu.VMEM((height, channels, columns), BF),
            pltpu.SemaphoreType.DMA,
        ],
        input_output_aliases=alias,
        compiler_params=pltpu.CompilerParams(vmem_limit_bytes=VMEM_BYTES),
        cost_estimate=pl.CostEstimate(
            flops=18 * height * channels * channels * columns, bytes_accessed=4 << 20, transcendentals=0
        ),
        name="back",
    )(*args)


def weight_kernel(height, scale, spot, up, top, mid, bot, down, saved, own, one, two, three, shift_ref):
    channels = top.shape[0]
    rows = [up[...], top[...], *[mid[i] for i in range(height - 2)], bot[...], down[...]]
    fill_shifted(shift_ref, rows)
    inputs = [jnp.maximum(saved[r], 0) for r in range(height)]
    part = channels // 4
    piece = part // 4
    for k, out in enumerate((own, one, two, three)):
        place = lax.rem(spot[0] + k, 4)
        start = pl.multiple_of(place * part, part)
        total = None
        for r in range(height):
            left = shift_ref[:, r : r + 3, pl.ds(start, part), :].reshape(9 * part, -1)
            term = lax.dot_general(left, inputs[r], (((1,), (1,)), ((), ())), preferred_element_type=F32)
            total = term if total is None else total + term
        total = total * scale
        for b in range(3):
            for j in range(3):
                base = (3 * b + j) * part
                for q in range(4):
                    out[q, 3 * (2 - j) + b] = total[base + q * piece : base + (q + 1) * piece].astype(out.dtype)


def weight_terms(edges, saved, spot, scale):
    height, channels, columns = saved.shape
    part = (4, 9, channels // 16, channels)
    return pl.pallas_call(
        functools.partial(weight_kernel, height, scale),
        out_shape=[jax.ShapeDtypeStruct(part, F32)] + [jax.ShapeDtypeStruct(part, BF)] * 3,
        in_specs=[whole(pltpu.SMEM)] + [whole()] * 6,
        out_specs=[whole()] * 4,
        scratch_shapes=[pltpu.VMEM((3, height + 2, channels, columns), BF)],
        compiler_params=pltpu.CompilerParams(vmem_limit_bytes=VMEM_BYTES),
        cost_estimate=pl.CostEstimate(
            flops=18 * height * channels * channels * columns, bytes_accessed=4 << 20, transcendentals=0
        ),
        name="weight",
    )(spot, *edges, saved)


def regroup_kernel(spot, own, one, two, three, mine, first, second, third):
    for k, out in enumerate((mine, first, second, third)):
        place = lax.rem(spot[0] + k, 4)
        value = (own[place] + one[place].astype(F32)) + (two[place].astype(F32) + three[place].astype(F32))
        out[...] = value.astype(out.dtype)


def regroup(spot, parts):
    shape = parts[0].shape[1:]
    return pl.pallas_call(
        regroup_kernel,
        out_shape=[jax.ShapeDtypeStruct(shape, F32)] + [jax.ShapeDtypeStruct(shape, BF)] * 3,
        in_specs=[whole(pltpu.SMEM)] + [whole()] * 4,
        out_specs=[whole()] * 4,
        compiler_params=pltpu.CompilerParams(vmem_limit_bytes=VMEM_BYTES),
        name="regroup",
    )(spot, *parts)


def finish_kernel(held, own, one, two, three, out):
    value = (own[...] + one[...].astype(F32)) + (two[...].astype(F32) + three[...].astype(F32))
    out[...] = (held[...].astype(F32) + value).astype(BF)


def finish(held, parts):
    return pl.pallas_call(
        finish_kernel,
        out_shape=jax.ShapeDtypeStruct(held.shape, BF),
        in_specs=[whole()] * 5,
        out_specs=whole(),
        name="finish",
    )(held, *parts)


def along(value, move):
    return lax.ppermute(value, "rows", [(x * 4 + z, move(x, z)) for x in range(4) for z in range(4)])


def shifted(value, by):
    return lax.ppermute(value, "blk", [(i, (i + by) % 16) for i in range(16)])


def with_edges(top, mid, bot):
    up = lax.ppermute(bot, "rows", [(i, i + 1) for i in range(15)])
    down = lax.ppermute(top, "rows", [(i + 1, i) for i in range(15)])
    return up, top, mid, bot, down


def reduce_rows(parts, spot_z):
    moved = [parts[0]] + [
        along(parts[k], lambda x, z, k=k: ((x + k) % 4) * 4 + z) for k in (2, 1, 3)
    ]
    pieces = regroup(spot_z, moved)
    return [pieces[0]] + [
        along(pieces[k], lambda x, z, k=k: x * 4 + (z + k) % 4) for k in (2, 1, 3)
    ]


def shards(section_weights, grad_acc, saved_inputs, cotangent, fresh_grads):
    position = lax.axis_index("blk")
    row = lax.axis_index("rows")
    spot_x = (row // 4).reshape(1)
    spot_z = (row % 4).reshape(1)
    kernel = jnp.transpose(section_weights[0], (1, 0, 2))
    held = jnp.transpose(grad_acc[0], (1, 0, 2))
    height = cotangent.shape[1]
    columns = cotangent.shape[3]
    scale = float(16 * height * columns) ** (-0.5)
    image = cotangent[0]
    edges = with_edges(image[0], image[1 : height - 1], image[height - 1])
    kernels = [kernel, shifted(kernel, -1), shifted(kernel, -2)]
    states = None
    for tick in range(TICKS):
        saved = saved_inputs[tick, 0]
        now = edges
        if tick + 1 < TICKS:
            restart = (position == 16 - tick - 1).astype(jnp.int32).reshape(1)
            states, *parts = back_project(tick, now, kernels[tick], saved, states, restart, fresh_grads[tick])
            edges = with_edges(*parts)
        else:
            (states,) = back_project(tick, now, kernels[tick], saved, states, None, None)
        sums = reduce_rows(weight_terms(now, saved, spot_x, scale), spot_z)
        held = finish(held, sums)
        if tick + 1 < TICKS:
            held = shifted(held, -1)
    return states, jnp.transpose(held, (1, 0, 2))[None]


def solution(mesh):
    return jax.shard_map(
        shards,
        mesh=mesh,
        in_specs=(
            P("blk", None, None, None),
            P("blk", "rows", None, None),
            P(None, "blk", "rows", None, None),
            P("blk", "rows", None, None),
            P(None, "rows", None, None),
        ),
        out_specs=(P(None, "blk", "rows", None, None), P("blk", "rows", None, None)),
        check_vma=False,
    )
```

```python
import functools

import jax
import jax.numpy as jnp
from jax import lax
from jax.experimental import pallas as pl
from jax.experimental.pallas import tpu as pltpu
from jax.sharding import PartitionSpec as P

TICKS = 3
BF = jnp.bfloat16
F32 = jnp.float32
VMEM_BYTES = 12 * 1024 * 1024
SMALL_VMEM_BYTES = 4 * 1024 * 1024


def whole(memory=pltpu.VMEM):
    return pl.BlockSpec(memory_space=memory)


def fill_shifted(shift_ref, rows):
    for index, row in enumerate(rows):
        wide = row.astype(F32)
        columns = wide.shape[1]
        place = lax.broadcasted_iota(jnp.int32, wide.shape, 1)
        ahead = pltpu.roll(wide, columns - 1, 1)
        behind = pltpu.roll(wide, 1, 1)
        shift_ref[0, index] = jnp.where(place == columns - 1, 0.0, ahead).astype(BF)
        shift_ref[1, index] = row
        shift_ref[2, index] = jnp.where(place == 0, 0.0, behind).astype(BF)


def back_kernel(tick, height, *refs):
    refs = list(refs)
    last = tick == TICKS - 1
    flag = None if last else refs.pop(0)
    spot = refs.pop(0) if tick > 0 else None
    up, top, mid, bot, down, kernel, saved = refs[:7]
    refs = refs[7:]
    if tick > 0:
        pieces = refs[:4]
        refs = refs[4:]
    fresh = None if last else refs.pop(0)
    if tick > 0:
        refs.pop(0)
    states = refs.pop(0)
    if not last:
        next_top, next_mid, next_bot = refs[:3]
        refs = refs[3:]
    if tick > 0:
        joined = refs.pop(0)
        part = pieces[0].shape[1]
        for k in range(4):
            start = pl.multiple_of(lax.rem(spot[0] + k, 4) * part, part)
            joined[:, pl.ds(start, part), :] = kernel[:, pl.ds(start, part), :] + pieces[k][...]
        kernel = joined
    shift_ref, turned, result, sem = refs
    channels = top.shape[0]
    rows = [up[...], top[...], *[mid[i] for i in range(height - 2)], bot[...], down[...]]
    fill_shifted(shift_ref, rows)
    for b in range(3):
        for j in range(3):
            turned[b, :, j * channels : (j + 1) * channels] = kernel[3 * (2 - j) + b].T
    for r in range(height):
        total = None
        for b in range(3):
            window = shift_ref[b, r : r + 3].reshape(3 * channels, -1)
            part = jnp.dot(turned[b], window, preferred_element_type=F32)
            total = part if total is None else total + part
        value = jnp.where(saved[r] > 0, total, 0.0).astype(BF)
        result[r] = value
        if not last:
            value = jnp.where(flag[0] > 0, fresh[r], value)
            if r == 0:
                next_top[...] = value
            elif r == height - 1:
                next_bot[...] = value
            else:
                next_mid[r - 1] = value
    copy = pltpu.make_async_copy(result, states.at[tick, 0], sem)
    copy.start()
    copy.wait()


def back_project(tick, edges, kernel, pieces, saved, states, restart, fresh, spot):
    last = tick == TICKS - 1
    height, channels, columns = saved.shape
    args, specs = [], []

    def give(value, memory=pltpu.VMEM):
        args.append(value)
        specs.append(whole(memory))

    if not last:
        give(restart, pltpu.SMEM)
    if tick > 0:
        give(spot, pltpu.SMEM)
    for value in (*edges, kernel, saved):
        give(value)
    if tick > 0:
        for value in pieces:
            give(value)
    if not last:
        give(fresh)
    alias = {}
    if tick > 0:
        alias = {len(args): 0}
        give(states, pl.ANY)
    shapes = [jax.ShapeDtypeStruct((TICKS, 1, height, channels, columns), BF)]
    scratch = [
        pltpu.VMEM((3, height + 2, channels, columns), BF),
        pltpu.VMEM((3, channels, 3 * channels), BF),
        pltpu.VMEM((height, channels, columns), BF),
        pltpu.SemaphoreType.DMA,
    ]
    if not last:
        shapes += [
            jax.ShapeDtypeStruct((channels, columns), BF),
            jax.ShapeDtypeStruct((height - 2, channels, columns), BF),
            jax.ShapeDtypeStruct((channels, columns), BF),
        ]
        if tick > 0:
            shapes.append(jax.ShapeDtypeStruct(kernel.shape, BF))
    else:
        scratch = [pltpu.VMEM(kernel.shape, BF)] + scratch
    return pl.pallas_call(
        functools.partial(back_kernel, tick, height),
        out_shape=shapes,
        in_specs=specs,
        out_specs=[whole(pl.ANY)] + [whole()] * (len(shapes) - 1),
        scratch_shapes=scratch,
        input_output_aliases=alias,
        compiler_params=pltpu.CompilerParams(vmem_limit_bytes=VMEM_BYTES),
        cost_estimate=pl.CostEstimate(
            flops=18 * height * channels * channels * columns, bytes_accessed=4 << 20, transcendentals=0
        ),
        name="back",
    )(*args)


def weight_kernel(tick, height, scale, *refs):
    refs = list(refs)
    spot = refs.pop(0) if tick > 0 else None
    even = refs.pop(0) if tick == 1 else None
    up, top, mid, bot, down, saved = refs[:6]
    refs = refs[6:]
    other = refs.pop(0) if tick > 0 else None
    shift_ref = refs.pop()
    channels = top.shape[0]
    rows = [up[...], top[...], *[mid[i] for i in range(height - 2)], bot[...], down[...]]
    fill_shifted(shift_ref, rows)
    inputs = [jnp.maximum(saved[r], 0) for r in range(height)]
    part = channels // 4
    piece = part // 4
    for k in range(4):
        place = lax.rem(spot[0] + k, 4) if tick > 0 else k
        start = pl.multiple_of(place * part, part) if tick > 0 else k * part
        total = None
        for r in range(height):
            left = shift_ref[:, r : r + 3, pl.ds(start, part), :].reshape(9 * part, -1)
            term = lax.dot_general(left, inputs[r], (((1,), (1,)), ((), ())), preferred_element_type=F32)
            total = term if total is None else total + term
        total = total * scale
        for b in range(3):
            for j in range(3):
                base = (3 * b + j) * part
                tap = 3 * (2 - j) + b
                for q in range(4):
                    value = total[base + q * piece : base + (q + 1) * piece]
                    if tick == 0:
                        refs[0][k, q, tap] = value.astype(BF)
                        continue
                    out = refs[k]
                    if tick == 1:
                        refs[4][place, q, tap] = value.astype(BF)
                        value = jnp.where(even[0] > 0, value, 0.0)
                    out[q, tap] = (value + other[place, q, tap].astype(F32)).astype(out.dtype)


def weight_terms(tick, edges, saved, scale, spot=None, even=None, other=None):
    height, channels, columns = saved.shape
    part = (4, 9, channels // 16, channels)
    full = jax.ShapeDtypeStruct((4, *part), BF)
    shapes = [jax.ShapeDtypeStruct(part, F32)] + [jax.ShapeDtypeStruct(part, BF)] * 3
    scalars = [[], [spot, even], [spot]][tick]
    rest = [*edges, saved] + ([other] if tick > 0 else [])
    return pl.pallas_call(
        functools.partial(weight_kernel, tick, height, scale),
        out_shape=[[full], shapes + [full], shapes][tick],
        in_specs=[whole(pltpu.SMEM)] * len(scalars) + [whole()] * len(rest),
        out_specs=[whole()] * (1, 5, 4)[tick],
        scratch_shapes=[pltpu.VMEM((3, height + 2, channels, columns), BF)],
        compiler_params=pltpu.CompilerParams(vmem_limit_bytes=VMEM_BYTES),
        cost_estimate=pl.CostEstimate(
            flops=18 * height * channels * channels * columns, bytes_accessed=4 << 20, transcendentals=0
        ),
        name="weight",
    )(*scalars, *rest)


def regroup_kernel(spot, own, one, two, three, mine, first, second, third):
    for k, out in enumerate((mine, first, second, third)):
        place = lax.rem(spot[0] + k, 4)
        value = (own[place] + one[place].astype(F32)) + (two[place].astype(F32) + three[place].astype(F32))
        out[...] = value.astype(out.dtype)


def regroup(spot, parts):
    shape = parts[0].shape[1:]
    return pl.pallas_call(
        regroup_kernel,
        out_shape=[jax.ShapeDtypeStruct(shape, F32)] + [jax.ShapeDtypeStruct(shape, BF)] * 3,
        in_specs=[whole(pltpu.SMEM)] + [whole()] * 4,
        out_specs=[whole()] * 4,
        compiler_params=pltpu.CompilerParams(vmem_limit_bytes=SMALL_VMEM_BYTES),
        name="regroup",
    )(spot, *parts)


def total_of(own, one, two, three):
    return (own[...] + one[...].astype(F32)) + (two[...].astype(F32) + three[...].astype(F32))


def collect_kernel(own, one, two, three, out):
    out[...] = total_of(own, one, two, three).astype(BF)


def finish_kernel(held, early, own, one, two, three, out):
    out[...] = (held[...].astype(F32) + early[...].astype(F32) + total_of(own, one, two, three)).astype(BF)


def finish(parts, *before):
    return pl.pallas_call(
        finish_kernel if before else collect_kernel,
        out_shape=jax.ShapeDtypeStruct(parts[0].shape, BF),
        in_specs=[whole()] * (4 + len(before)),
        out_specs=whole(),
        compiler_params=pltpu.CompilerParams(vmem_limit_bytes=SMALL_VMEM_BYTES),
        name="finish",
    )(*before, *parts)


def along(value, move):
    return lax.ppermute(value, "rows", [(x * 4 + z, move(x, z)) for x in range(4) for z in range(4)])


def along_odd(value, move):
    pairs = [(b * 16 + x * 4 + z, b * 16 + move(x, z)) for b in range(1, 16, 2) for x in range(4) for z in range(4)]
    return lax.ppermute(value, ("blk", "rows"), pairs)


def around(value, pairs):
    return lax.ppermute(value, "blk", pairs)


def with_edges(top, mid, bot):
    up = lax.ppermute(bot, "rows", [(i, i + 1) for i in range(15)])
    down = lax.ppermute(top, "rows", [(i + 1, i) for i in range(15)])
    return up, top, mid, bot, down


def gathered(own):
    return [own] + [along_odd(own, lambda x, z, k=k: ((x - k) % 4) * 4 + z) for k in (1, 2, 3)]


def reduce_rows(parts, spot_z):
    moved = [parts[0]] + [along(parts[k], lambda x, z, k=k: ((x + k) % 4) * 4 + z) for k in (1, 2, 3)]
    pieces = regroup(spot_z, moved)
    return [pieces[0]] + [along(pieces[k], lambda x, z, k=k: x * 4 + (z + k) % 4) for k in (1, 2, 3)]


def shards(section_weights, grad_acc, saved_inputs, cotangent, fresh_grads):
    position = lax.axis_index("blk")
    row = lax.axis_index("rows")
    spot_x = (row // 4).reshape(1)
    spot_z = (row % 4).reshape(1)
    even = (position % 2 == 0).astype(jnp.int32).reshape(1)
    kernel = jnp.transpose(section_weights[0], (1, 0, 2))
    held = jnp.transpose(grad_acc[0], (1, 0, 2))
    height = cotangent.shape[1]
    channels = cotangent.shape[2]
    columns = cotangent.shape[3]
    scale = float(16 * height * columns) ** (-0.5)
    evens = range(0, 16, 2)
    down_core = [(b + 1, b) for b in evens]
    image = cotangent[0]
    edges = with_edges(image[0], image[1 : height - 1], image[height - 1])
    quarter = lax.dynamic_slice_in_dim(kernel, spot_x[0] * (channels // 4), channels // 4, 1)
    pieces_one = gathered(around(quarter, [(b, (b - 1) % 16) for b in evens]))
    kernel_one = around(kernel, down_core)

    def back(tick, edges, kernel, pieces, states):
        restart = (position == 16 - tick - 1).astype(jnp.int32).reshape(1)
        fresh = fresh_grads[tick] if tick + 1 < TICKS else None
        return back_project(tick, edges, kernel, pieces, saved_inputs[tick, 0], states, restart, fresh, spot_x)

    states, *parts = back(0, edges, kernel, None, None)
    edges_one = with_edges(*parts)
    (sums,) = weight_terms(0, edges, saved_inputs[0, 0], scale)
    other = around(sums, [(b, b ^ 1) for b in range(16)])
    states, *parts, used = back(1, edges_one, kernel_one, pieces_one, states)
    edges_two = with_edges(*parts)
    *parts, sums = weight_terms(1, edges_one, saved_inputs[1, 0], scale, spot_x, even, other)
    other = around(sums, down_core)
    early = finish(reduce_rows(parts, spot_z))
    held = around(held, [(b, (b - 2) % 16) for b in range(16)])
    early = around(early, [(b, (b - 1) % 16) for b in evens] + [(b + 1, (b - 2) % 16) for b in evens])
    parts = weight_terms(2, edges_two, saved_inputs[2, 0], scale, spot_x, even, other)
    pieces_two = gathered(around(quarter, [(b + 1, (b - 1) % 16) for b in evens]))
    kernel_two = around(used, down_core)
    (states,) = back(2, edges_two, kernel_two, pieces_two, states)
    held = finish(reduce_rows(parts, spot_z), held, early)
    return states, jnp.transpose(held, (1, 0, 2))[None]


def solution(mesh):
    return jax.shard_map(
        shards,
        mesh=mesh,
        in_specs=(
            P("blk", None, None, None),
            P("blk", "rows", None, None),
            P(None, "blk", "rows", None, None),
            P("blk", "rows", None, None),
            P(None, "rows", None, None),
        ),
        out_specs=(P(None, "blk", "rows", None, None), P("blk", "rows", None, None)),
        check_vma=False,
    )
```

```python
import functools

import jax
import jax.numpy as jnp
from jax import lax
from jax.experimental import pallas as pl
from jax.experimental.pallas import tpu as pltpu
from jax.sharding import PartitionSpec as P

TICKS = 3
BF = jnp.bfloat16
F32 = jnp.float32
VMEM_BYTES = 12 * 1024 * 1024
SMALL_VMEM_BYTES = 6 * 1024 * 1024


def whole(memory=pltpu.VMEM):
    return pl.BlockSpec(memory_space=memory)


def fill_shifted(shift_ref, rows):
    for index, row in enumerate(rows):
        wide = row.astype(F32)
        columns = wide.shape[1]
        place = lax.broadcasted_iota(jnp.int32, wide.shape, 1)
        ahead = pltpu.roll(wide, columns - 1, 1)
        behind = pltpu.roll(wide, 1, 1)
        shift_ref[0, index] = jnp.where(place == columns - 1, 0.0, ahead).astype(BF)
        shift_ref[1, index] = row
        shift_ref[2, index] = jnp.where(place == 0, 0.0, behind).astype(BF)


def near(shape, kind=BF):
    return jax.ShapeDtypeStruct(shape, kind)


def kept(value):
    return pltpu.with_memory_space_constraint(value, pltpu.HBM)


def fetch(pairs, sems):
    copies = [pltpu.make_async_copy(source, target, sems.at[i]) for i, (source, target) in enumerate(pairs)]
    for copy in copies:
        copy.start()
    return copies


def gradient_rows(edges, image):
    if image is None:
        up, top, mid, bot, down = edges
        return [up[...], top[...], *[mid[i] for i in range(mid.shape[0])], bot[...], down[...]]
    return [edges[0][...], *[image[i] for i in range(image.shape[0])], edges[1][...]]


def back_kernel(tick, *refs):
    refs = list(refs)
    first, last = tick == 0, tick == TICKS - 1
    restart = lax.axis_index("blk") == lax.axis_size("blk") - tick - 1
    edges = [refs.pop(0) for _ in range(2 if first else 5)]
    image_far = refs.pop(0) if first else None
    kernel = refs.pop(0)
    pieces = [refs.pop(0) for _ in range(2)] if tick == 1 else []
    saved_far = refs.pop(0)
    fresh_far = None if last else refs.pop(0)
    if not first:
        refs.pop(0)
    states = refs.pop(0)
    outs = [] if last else [refs.pop(0) for _ in range(3)]
    joined = kernel if last else refs.pop(0)
    shift_ref, turned, result, saved = [refs.pop(0) for _ in range(4)]
    fresh = None if last else refs.pop(0)
    image = refs.pop(0) if first else None
    sems, sem = refs
    height, channels, _ = saved.shape
    pairs = [(saved_far.at[tick, 0], saved)]
    if first:
        pairs = [(image_far.at[0], image), (kernel, joined)] + pairs
    if not last:
        pairs.append((fresh_far.at[tick], fresh))
    copies = fetch(pairs, sems)
    if first:
        copies.pop(0).wait()
    fill_shifted(shift_ref, gradient_rows(edges, image))
    if first:
        copies.pop(0).wait()
    for k, piece in enumerate(pieces):
        part = piece.shape[1]
        start = pl.multiple_of(lax.rem(lax.axis_index("rows") // 4 + k, 2) * part, part)
        joined[:, pl.ds(start, part), :] = kernel[:, pl.ds(start, part), :] + piece[...]
    for b in range(3):
        for j in range(3):
            turned[b, :, j * channels : (j + 1) * channels] = joined[3 * (2 - j) + b].T
    for copy in copies:
        copy.wait()
    copies = []
    for r in range(height):
        total = None
        for b in range(3):
            window = shift_ref[b, r : r + 3].reshape(3 * channels, -1)
            part = jnp.dot(turned[b], window, preferred_element_type=F32)
            total = part if total is None else total + part
        value = jnp.where(saved[r] > 0, total, 0.0).astype(BF)
        result[r] = value
        copy = pltpu.make_async_copy(result.at[r], states.at[tick, 0, r], sem.at[r])
        copy.start()
        copies.append(copy)
        if not last:
            value = jnp.where(restart, fresh[r], value)
            if r == 0:
                outs[0][...] = value
            elif r == height - 1:
                outs[2][...] = value
            else:
                outs[1][r - 1] = value
    for copy in copies:
        copy.wait()


def back_project(tick, edges, image, kernel, pieces, saved, states, fresh):
    first, last = tick == 0, tick == TICKS - 1
    _, _, height, channels, columns = saved.shape
    args, specs = [], []

    def give(value, memory=pltpu.VMEM):
        args.append(kept(value) if memory is pl.ANY else value)
        specs.append(whole(memory))

    for value in edges:
        give(value)
    if first:
        give(image, pl.ANY)
        give(kernel, pl.ANY)
    else:
        for value in (kernel, *pieces):
            give(value)
    give(saved, pl.ANY)
    if not last:
        give(fresh, pl.ANY)
    alias = {}
    if not first:
        alias = {len(args): 0}
        give(states, pl.ANY)
    shapes = [jax.ShapeDtypeStruct((TICKS, 1, height, channels, columns), BF)]
    block = (height, channels, columns)
    scratch = [
        pltpu.VMEM((3, height + 2, channels, columns), BF),
        pltpu.VMEM((3, channels, 3 * channels), BF),
        pltpu.VMEM(block, BF),
        pltpu.VMEM(block, BF),
    ]
    if not last:
        shapes += [near((channels, columns)), near((height - 2, channels, columns)), near((channels, columns))]
        scratch.append(pltpu.VMEM(block, BF))
    if first:
        scratch.append(pltpu.VMEM(block, BF))
    if tick == 1:
        shapes.append(near(kernel.shape))
    if first:
        scratch = [pltpu.VMEM(kernel.shape, BF)] + scratch
    scratch += [pltpu.SemaphoreType.DMA((4,)), pltpu.SemaphoreType.DMA((height,))]
    return pl.pallas_call(
        functools.partial(back_kernel, tick),
        out_shape=shapes,
        in_specs=specs,
        out_specs=[whole(pl.ANY)] + [whole()] * (len(shapes) - 1),
        scratch_shapes=scratch,
        input_output_aliases=alias,
        compiler_params=pltpu.CompilerParams(vmem_limit_bytes=VMEM_BYTES),
        cost_estimate=pl.CostEstimate(flops=1, bytes_accessed=1, transcendentals=0),
        name="back",
    )(*args)


def weight_kernel(tick, scale, *refs):
    refs = list(refs)
    first = tick == 0
    edges = [refs.pop(0) for _ in range(2 if first else 5)]
    image_far = refs.pop(0) if first else None
    saved_far = refs.pop(0)
    out = refs.pop(0)
    sems = refs.pop()
    image = refs.pop() if first else None
    saved = refs.pop()
    shift_ref = refs.pop()
    height, channels, _ = saved.shape
    pairs = [(saved_far.at[tick, 0], saved)]
    if first:
        pairs.insert(0, (image_far.at[0], image))
    copies = fetch(pairs, sems)
    if first:
        copies.pop(0).wait()
    fill_shifted(shift_ref, gradient_rows(edges, image))
    copies.pop(0).wait()
    inputs = [jnp.maximum(saved[r], 0) for r in range(height)]
    part = channels // 4
    piece = part // 4
    for k in range(4):
        total = None
        for r in range(height):
            left = shift_ref[:, r : r + 3, k * part : (k + 1) * part, :].reshape(9 * part, -1)
            term = lax.dot_general(left, inputs[r], (((1,), (1,)), ((), ())), preferred_element_type=F32)
            total = term if total is None else total + term
        total = total * scale
        for b in range(3):
            for j in range(3):
                base = (3 * b + j) * part
                tap = 3 * (2 - j) + b
                for q in range(4):
                    value = total[base + q * piece : base + (q + 1) * piece]
                    out[k, q, tap] = value.astype(BF)


def weight_terms(tick, edges, image, saved, scale):
    _, _, height, channels, columns = saved.shape
    rest = [(edge, pltpu.VMEM) for edge in edges]
    if tick == 0:
        rest.append((kept(image), pl.ANY))
    rest.append((kept(saved), pl.ANY))
    block = pltpu.VMEM((height, channels, columns), BF)
    return pl.pallas_call(
        functools.partial(weight_kernel, tick, scale),
        out_shape=near((4, 4, 9, channels // 16, channels)),
        in_specs=[whole(memory) for _, memory in rest],
        out_specs=whole(),
        scratch_shapes=[pltpu.VMEM((3, height + 2, channels, columns), BF)]
        + [block] * (2 if tick == 0 else 1)
        + [pltpu.SemaphoreType.DMA((2,))],
        compiler_params=pltpu.CompilerParams(vmem_limit_bytes=VMEM_BYTES),
        cost_estimate=pl.CostEstimate(flops=1, bytes_accessed=1, transcendentals=0),
        name="weight",
    )(*[value for value, _ in rest])


def half_kernel(kernel, out, sem):
    part = out.shape[1]
    start = pl.multiple_of(lax.rem(lax.axis_index("rows") // 4, 2) * part, part)
    copy = pltpu.make_async_copy(kernel.at[:, pl.ds(start, part), :], out, sem)
    copy.start()
    copy.wait()


def half_of(kernel):
    taps, rows, columns = kernel.shape
    return pl.pallas_call(
        half_kernel,
        out_shape=near((taps, rows // 2, columns)),
        in_specs=[whole(pl.ANY)],
        out_specs=whole(),
        scratch_shapes=[pltpu.SemaphoreType.DMA],
        compiler_params=pltpu.CompilerParams(vmem_limit_bytes=SMALL_VMEM_BYTES),
        name="half",
    )(kept(kernel))


def pair_kernel(zero, two, other, *outs):
    odd = lax.axis_index("blk") % 2 == 1
    for k in range(4):
        place = lax.rem(lax.axis_index("rows") // 4 + k, 4)
        for q in range(4):
            more = other[place, q].astype(F32)
            early = zero[place, q].astype(F32) + jnp.where(odd, more, 0.0)
            late = two[place, q].astype(F32) + jnp.where(odd, 0.0, more)
            outs[k][q] = early.astype(outs[k].dtype)
            outs[4 + k][q] = late.astype(outs[4 + k].dtype)


def regroup_kernel(own, one, two, three, keep, send):
    place = lax.rem(lax.axis_index("rows"), 4)
    beside = place + 1 - 2 * lax.rem(place, 2)
    spots = (place, lax.rem(place + 2, 4), beside, lax.rem(beside + 2, 4))
    for k, spot in enumerate(spots):
        value = (own[spot] + one[spot].astype(F32)) + (two[spot].astype(F32) + three[spot].astype(F32))
        if k < 2:
            keep[k] = value
        else:
            send[k - 2] = value.astype(BF)


def halve_kernel(keep, came, kept_on, send):
    kept_on[...] = keep[0] + came[0].astype(F32)
    send[...] = (keep[1] + came[1].astype(F32)).astype(BF)


def finish_kernel(held, keep, came, out):
    out[...] = (held[...].astype(F32) + (keep[...] + came[...].astype(F32))).astype(BF)


def small(kernel, shapes, *args):
    return pl.pallas_call(
        kernel,
        out_shape=shapes,
        in_specs=[whole()] * len(args),
        out_specs=[whole()] * len(shapes),
        compiler_params=pltpu.CompilerParams(vmem_limit_bytes=SMALL_VMEM_BYTES),
        cost_estimate=pl.CostEstimate(flops=1, bytes_accessed=1, transcendentals=0),
        name=kernel.__name__,
    )(*args)


def after(values, *others):
    return lax.optimization_barrier((values, others))[0]


def along(value, move):
    return lax.ppermute(value, "rows", [(x * 4 + z, move(x, z)) for x in range(4) for z in range(4)])


def along_odd(value, move):
    pairs = [(b * 16 + x * 4 + z, b * 16 + move(x, z)) for b in range(1, 16, 2) for x in range(4) for z in range(4)]
    return lax.ppermute(value, ("blk", "rows"), pairs)


def around(value, pairs):
    return lax.ppermute(value, "blk", pairs)


def with_edges(top, mid, bot):
    up = lax.ppermute(bot, "rows", [(i, i + 1) for i in range(15)])
    down = lax.ppermute(top, "rows", [(i + 1, i) for i in range(15)])
    return up, top, mid, bot, down


def over_x(parts):
    return [parts[0]] + [along(parts[k], lambda x, z, k=k: ((x + k) % 4) * 4 + z) for k in (1, 2, 3)]


def part_over_z(parts, held):
    shape = (2, *held.shape)
    keep, send = small(regroup_kernel, [near(shape, F32), near(shape)], *parts)
    return keep, along(send, lambda x, z: x * 4 + (z ^ 1))


def rest_over_z(keep, came):
    shape = keep.shape[1:]
    keep, send = small(halve_kernel, [near(shape, F32), near(shape)], keep, came)
    return keep, along(send, lambda x, z: x * 4 + (z ^ 2))


def summed_over_z(parts, held):
    return rest_over_z(*part_over_z(parts, held))


def shards(section_weights, grad_acc, saved_inputs, cotangent, fresh_grads):
    kernel = jnp.transpose(section_weights[0], (1, 0, 2))
    held = jnp.transpose(grad_acc[0], (1, 0, 2))
    height = cotangent.shape[1]
    columns = cotangent.shape[3]
    scale = float(16 * height * columns) ** (-0.5)
    image = cotangent[0]
    back_by = lambda by: [(b, (b - by) % 16) for b in range(16)]
    evens = range(0, 16, 2)

    def back(tick, edges, kernel, pieces, states):
        return back_project(tick, edges, cotangent, kernel, pieces, saved_inputs, states, fresh_grads)

    def weight(tick, edges):
        return weight_terms(tick, edges, cotangent, saved_inputs, scale)

    half = around(half_of(kernel), [(b, (b - 1) % 16) for b in evens])
    up, _, _, _, down = with_edges(image[0], None, image[height - 1])
    half, kernel_here = after((half, kernel), up, down)
    kernel_one = around(kernel_here, [(b + 1, b) for b in evens])
    states, *parts = back(0, (up, down), kernel, (), None)
    edges_one = with_edges(*parts)
    halves = [half, along_odd(half, lambda x, z: (x ^ 1) * 4 + z)]
    sums_zero = weight(0, after((up, down), parts[0]))
    edges_one = after(edges_one, sums_zero)
    states, *parts, used = back(1, edges_one, kernel_one, halves, states)
    edges_two = with_edges(*parts)
    sums_one = weight(1, after(edges_one, parts[0]))
    edges_two, used, sums_one = lax.optimization_barrier((edges_two, used, sums_one))
    other = around(sums_one, [(b, b ^ 1) for b in range(16)])
    kernel_two = around(used, back_by(1))
    sums_two = weight(2, edges_two)
    part = (4, *held.shape)
    spread = ([near(part, F32)] + [near(part)] * 3) * 2
    both = small(pair_kernel, spread, sums_zero, sums_two, other)
    first, last = over_x(both[:4]), over_x(both[4:])
    early = small(finish_kernel, [near(held.shape)], held, *summed_over_z(first, held))
    early = around(early[0], back_by(2))
    keep, came = part_over_z(last, held)
    (states,) = back(2, edges_two, kernel_two, (), states)
    came = after(came, states)
    (held,) = small(finish_kernel, [near(held.shape)], early, *rest_over_z(keep, came))
    return states, jnp.transpose(held, (1, 0, 2))[None]


def solution(mesh):
    return jax.shard_map(
        shards,
        mesh=mesh,
        in_specs=(
            P("blk", None, None, None),
            P("blk", "rows", None, None),
            P(None, "blk", "rows", None, None),
            P("blk", "rows", None, None),
            P(None, "rows", None, None),
        ),
        out_specs=(P(None, "blk", "rows", None, None), P("blk", "rows", None, None)),
        check_vma=False,
    )
```

```python
import functools

import jax
import jax.numpy as jnp
from jax import lax
from jax.experimental import pallas as pl
from jax.experimental.pallas import tpu as pltpu
from jax.sharding import PartitionSpec as P

TICKS = 3
BF = jnp.bfloat16
F32 = jnp.float32
VMEM_BYTES = 12 * 1024 * 1024
SMALL_VMEM_BYTES = 6 * 1024 * 1024


def whole(memory=pltpu.VMEM):
    return pl.BlockSpec(memory_space=memory)


def fill_shifted(shift_ref, rows):
    for index, row in enumerate(rows):
        wide = row.astype(F32)
        columns = wide.shape[1]
        place = lax.broadcasted_iota(jnp.int32, wide.shape, 1)
        ahead = pltpu.roll(wide, columns - 1, 1)
        behind = pltpu.roll(wide, 1, 1)
        shift_ref[0, index] = jnp.where(place == columns - 1, 0.0, ahead).astype(BF)
        shift_ref[1, index] = row
        shift_ref[2, index] = jnp.where(place == 0, 0.0, behind).astype(BF)


def near(shape, kind=BF):
    return jax.ShapeDtypeStruct(shape, kind)


def kept(value):
    return pltpu.with_memory_space_constraint(value, pltpu.HBM)


def fetch(pairs, sems):
    copies = [pltpu.make_async_copy(source, target, sems.at[i]) for i, (source, target) in enumerate(pairs)]
    for copy in copies:
        copy.start()
    return copies


def gradient_rows(edges, image):
    if image is None:
        up, top, mid, bot, down = edges
        return [up[...], top[...], *[mid[i] for i in range(mid.shape[0])], bot[...], down[...]]
    return [edges[0][...], *[image[i] for i in range(image.shape[0])], edges[1][...]]


def back_kernel(tick, *refs):
    refs = list(refs)
    first, last = tick == 0, tick == TICKS - 1
    restart = lax.axis_index("blk") == lax.axis_size("blk") - tick - 1
    edges = [refs.pop(0) for _ in range(2 if first else 5)]
    image_far = refs.pop(0) if first else None
    kernel = refs.pop(0)
    pieces = [refs.pop(0) for _ in range(2)] if tick == 1 else []
    saved_far = refs.pop(0)
    fresh_far = None if last else refs.pop(0)
    if not first:
        refs.pop(0)
    states = refs.pop(0)
    outs = [] if last else [refs.pop(0) for _ in range(3)]
    joined = kernel if last else refs.pop(0)
    shift_ref, turned, result, saved = [refs.pop(0) for _ in range(4)]
    fresh = None if last else refs.pop(0)
    image = refs.pop(0) if first else None
    sems, sem = refs
    height, channels, _ = saved.shape
    pairs = [(saved_far.at[tick, 0], saved)]
    if first:
        pairs = [(image_far.at[0], image), (kernel, joined)] + pairs
    if not last:
        pairs.append((fresh_far.at[tick], fresh))
    copies = fetch(pairs, sems)
    if first:
        copies.pop(0).wait()
    fill_shifted(shift_ref, gradient_rows(edges, image))
    if first:
        copies.pop(0).wait()
    for k, piece in enumerate(pieces):
        part = piece.shape[1]
        start = pl.multiple_of(lax.rem(lax.axis_index("rows") // 4 + k, 2) * part, part)
        joined[:, pl.ds(start, part), :] = kernel[:, pl.ds(start, part), :] + piece[...]
    for b in range(3):
        for j in range(3):
            turned[b, :, j * channels : (j + 1) * channels] = joined[3 * (2 - j) + b].T
    for copy in copies:
        copy.wait()
    copies = []
    for r in range(height):
        total = None
        for b in range(3):
            window = shift_ref[b, r : r + 3].reshape(3 * channels, -1)
            part = jnp.dot(turned[b], window, preferred_element_type=F32)
            total = part if total is None else total + part
        value = jnp.where(saved[r] > 0, total, 0.0).astype(BF)
        result[r] = value
        copy = pltpu.make_async_copy(result.at[r], states.at[tick, 0, r], sem.at[r])
        copy.start()
        copies.append(copy)
        if not last:
            value = jnp.where(restart, fresh[r], value)
            if r == 0:
                outs[0][...] = value
            elif r == height - 1:
                outs[2][...] = value
            else:
                outs[1][r - 1] = value
    for copy in copies:
        copy.wait()


def back_project(tick, edges, image, kernel, pieces, saved, states, fresh):
    first, last = tick == 0, tick == TICKS - 1
    _, _, height, channels, columns = saved.shape
    args, specs = [], []

    def give(value, memory=pltpu.VMEM):
        args.append(kept(value) if memory is pl.ANY else value)
        specs.append(whole(memory))

    for value in edges:
        give(value)
    if first:
        give(image, pl.ANY)
        give(kernel, pl.ANY)
    else:
        for value in (kernel, *pieces):
            give(value)
    give(saved, pl.ANY)
    if not last:
        give(fresh, pl.ANY)
    alias = {}
    if not first:
        alias = {len(args): 0}
        give(states, pl.ANY)
    shapes = [jax.ShapeDtypeStruct((TICKS, 1, height, channels, columns), BF)]
    block = (height, channels, columns)
    scratch = [
        pltpu.VMEM((3, height + 2, channels, columns), BF),
        pltpu.VMEM((3, channels, 3 * channels), BF),
        pltpu.VMEM(block, BF),
        pltpu.VMEM(block, BF),
    ]
    if not last:
        shapes += [near((channels, columns)), near((height - 2, channels, columns)), near((channels, columns))]
        scratch.append(pltpu.VMEM(block, BF))
    if first:
        scratch.append(pltpu.VMEM(block, BF))
    if tick == 1:
        shapes.append(near(kernel.shape))
    if first:
        scratch = [pltpu.VMEM(kernel.shape, BF)] + scratch
    scratch += [pltpu.SemaphoreType.DMA((4,)), pltpu.SemaphoreType.DMA((height,))]
    return pl.pallas_call(
        functools.partial(back_kernel, tick),
        out_shape=shapes,
        in_specs=specs,
        out_specs=[whole(pl.ANY)] + [whole()] * (len(shapes) - 1),
        scratch_shapes=scratch,
        input_output_aliases=alias,
        compiler_params=pltpu.CompilerParams(vmem_limit_bytes=VMEM_BYTES),
        cost_estimate=pl.CostEstimate(flops=1, bytes_accessed=1, transcendentals=0),
        name="back",
    )(*args)


def weight_kernel(tick, scale, *refs):
    refs = list(refs)
    first = tick == 0
    edges = [refs.pop(0) for _ in range(2 if first else 5)]
    image_far = refs.pop(0) if first else None
    saved_far = refs.pop(0)
    out = refs.pop(0)
    sems = refs.pop()
    image = refs.pop() if first else None
    saved = refs.pop()
    shift_ref = refs.pop()
    height, channels, _ = saved.shape
    pairs = [(saved_far.at[tick, 0], saved)]
    if first:
        pairs.insert(0, (image_far.at[0], image))
    copies = fetch(pairs, sems)
    if first:
        copies.pop(0).wait()
    fill_shifted(shift_ref, gradient_rows(edges, image))
    copies.pop(0).wait()
    inputs = [jnp.maximum(saved[r], 0) for r in range(height)]
    part = channels // 4
    piece = part // 4
    for k in range(4):
        total = None
        for r in range(height):
            left = shift_ref[:, r : r + 3, k * part : (k + 1) * part, :].reshape(9 * part, -1)
            term = lax.dot_general(left, inputs[r], (((1,), (1,)), ((), ())), preferred_element_type=F32)
            total = term if total is None else total + term
        total = total * scale
        for b in range(3):
            for j in range(3):
                base = (3 * b + j) * part
                tap = 3 * (2 - j) + b
                for q in range(4):
                    value = total[base + q * piece : base + (q + 1) * piece]
                    out[k, q, tap] = value.astype(BF)


def weight_terms(tick, edges, image, saved, scale):
    _, _, height, channels, columns = saved.shape
    rest = [(edge, pltpu.VMEM) for edge in edges]
    if tick == 0:
        rest.append((kept(image), pl.ANY))
    rest.append((kept(saved), pl.ANY))
    block = pltpu.VMEM((height, channels, columns), BF)
    return pl.pallas_call(
        functools.partial(weight_kernel, tick, scale),
        out_shape=near((4, 4, 9, channels // 16, channels)),
        in_specs=[whole(memory) for _, memory in rest],
        out_specs=whole(),
        scratch_shapes=[pltpu.VMEM((3, height + 2, channels, columns), BF)]
        + [block] * (2 if tick == 0 else 1)
        + [pltpu.SemaphoreType.DMA((2,))],
        compiler_params=pltpu.CompilerParams(vmem_limit_bytes=VMEM_BYTES),
        cost_estimate=pl.CostEstimate(flops=1, bytes_accessed=1, transcendentals=0),
        name="weight",
    )(*[value for value, _ in rest])


def half_kernel(kernel, out, sem):
    part = out.shape[1]
    start = pl.multiple_of(lax.rem(lax.axis_index("rows") // 4, 2) * part, part)
    copy = pltpu.make_async_copy(kernel.at[:, pl.ds(start, part), :], out, sem)
    copy.start()
    copy.wait()


def half_of(kernel):
    taps, rows, columns = kernel.shape
    return pl.pallas_call(
        half_kernel,
        out_shape=near((taps, rows // 2, columns)),
        in_specs=[whole(pl.ANY)],
        out_specs=whole(),
        scratch_shapes=[pltpu.SemaphoreType.DMA],
        compiler_params=pltpu.CompilerParams(vmem_limit_bytes=SMALL_VMEM_BYTES),
        name="half",
    )(kept(kernel))


def pair_kernel(zero, two, other, *outs):
    odd = lax.axis_index("blk") % 2 == 1
    for k in range(4):
        place = lax.rem(lax.axis_index("rows") // 4 + k, 4)
        for q in range(4):
            more = other[place, q].astype(F32)
            early = zero[place, q].astype(F32) + jnp.where(odd, more, 0.0)
            late = two[place, q].astype(F32) + jnp.where(odd, 0.0, more)
            outs[k][q] = early.astype(outs[k].dtype)
            outs[4 + k][q] = late.astype(outs[4 + k].dtype)


def regroup_kernel(own, one, two, three, keep, send):
    place = lax.rem(lax.axis_index("rows"), 4)
    beside = place + 1 - 2 * lax.rem(place, 2)
    spots = (place, lax.rem(place + 2, 4), beside, lax.rem(beside + 2, 4))
    for k, spot in enumerate(spots):
        value = (own[spot] + one[spot].astype(F32)) + (two[spot].astype(F32) + three[spot].astype(F32))
        if k < 2:
            keep[k] = value
        else:
            send[k - 2] = value.astype(BF)


def halve_kernel(keep, came, kept_on, send):
    kept_on[...] = keep[0] + came[0].astype(F32)
    send[...] = (keep[1] + came[1].astype(F32)).astype(BF)


def finish_kernel(held, keep, came, out):
    out[...] = (held[...].astype(F32) + (keep[...] + came[...].astype(F32))).astype(BF)


def small(kernel, shapes, *args):
    return pl.pallas_call(
        kernel,
        out_shape=shapes,
        in_specs=[whole()] * len(args),
        out_specs=[whole()] * len(shapes),
        compiler_params=pltpu.CompilerParams(vmem_limit_bytes=SMALL_VMEM_BYTES),
        cost_estimate=pl.CostEstimate(flops=1, bytes_accessed=1, transcendentals=0),
        name=kernel.__name__,
    )(*args)


def after(values, *others):
    return lax.optimization_barrier((values, others))[0]


def along(value, move):
    return lax.ppermute(value, "rows", [(x * 4 + z, move(x, z)) for x in range(4) for z in range(4)])


def along_odd(value, move):
    pairs = [(b * 16 + x * 4 + z, b * 16 + move(x, z)) for b in range(1, 16, 2) for x in range(4) for z in range(4)]
    return lax.ppermute(value, ("blk", "rows"), pairs)


def kernels_back(value, pairs):
    places = [(x * 4 + z, x * 4 + 3 - z, x * 4 + z) for x in range(4) for z in range(4)]
    moves = [(a * 16 + (far if a // 8 != b // 8 else here), b * 16 + there) for a, b in pairs for here, far, there in places]
    return lax.ppermute(value, ("blk", "rows"), moves)


def around(value, pairs):
    return lax.ppermute(value, "blk", pairs)


def with_edges(top, mid, bot):
    up = lax.ppermute(bot, "rows", [(i, i + 1) for i in range(15)])
    down = lax.ppermute(top, "rows", [(i + 1, i) for i in range(15)])
    return up, top, mid, bot, down


def over_x(parts):
    return [parts[0]] + [along(parts[k], lambda x, z, k=k: ((x + k) % 4) * 4 + z) for k in (1, 2, 3)]


def part_over_z(parts, held):
    shape = (2, *held.shape)
    keep, send = small(regroup_kernel, [near(shape, F32), near(shape)], *parts)
    return keep, along(send, lambda x, z: x * 4 + (z ^ 1))


def rest_over_z(keep, came):
    shape = keep.shape[1:]
    keep, send = small(halve_kernel, [near(shape, F32), near(shape)], keep, came)
    return keep, along(send, lambda x, z: x * 4 + (z ^ 2))


def shards(section_weights, grad_acc, saved_inputs, cotangent, fresh_grads):
    kernel = jnp.transpose(section_weights[0], (1, 0, 2))
    held = jnp.transpose(grad_acc[0], (1, 0, 2))
    height = cotangent.shape[1]
    columns = cotangent.shape[3]
    scale = float(16 * height * columns) ** (-0.5)
    image = cotangent[0]
    back_by = lambda by: [(b, (b - by) % 16) for b in range(16)]
    evens = range(0, 16, 2)

    def back(tick, edges, kernel, pieces, states):
        return back_project(tick, edges, cotangent, kernel, pieces, saved_inputs, states, fresh_grads)

    def weight(tick, edges):
        return weight_terms(tick, edges, cotangent, saved_inputs, scale)

    half = kernels_back(half_of(kernel), [(b, (b - 1) % 16) for b in evens])
    up, _, _, _, down = with_edges(image[0], None, image[height - 1])
    half, kernel_here = after((half, kernel), up, down)
    kernel_one = around(kernel_here, [(b + 1, b) for b in evens])
    states, *parts = back(0, (up, down), kernel, (), None)
    edges_one = with_edges(*parts)
    halves = [half, along_odd(half, lambda x, z: (x ^ 1) * 4 + z)]
    sums_zero = weight(0, after((up, down), parts[0]))
    edges_one = after(edges_one, sums_zero)
    states, *parts, used = back(1, edges_one, kernel_one, halves, states)
    edges_two = with_edges(*parts)
    sums_one = weight(1, after(edges_one, parts[0]))
    edges_two, used, sums_one = lax.optimization_barrier((edges_two, used, sums_one))
    other = around(sums_one, [(b, b ^ 1) for b in range(16)])
    kernel_two = kernels_back(used, back_by(1))
    sums_two = weight(2, edges_two)
    part = (4, *held.shape)
    spread = ([near(part, F32)] + [near(part)] * 3) * 2
    both = small(pair_kernel, spread, sums_zero, sums_two, other)
    first, last = over_x(both[:4]), over_x(both[4:])
    keep, came = part_over_z(first, held)
    (states,) = back(2, after(edges_two, keep), kernel_two, (), states)
    keep, came = rest_over_z(keep, after(came, states))
    last = after(last, keep)
    (early,) = small(finish_kernel, [near(held.shape)], held, keep, came)
    early = around(early, back_by(2))
    keep, came = part_over_z(last, held)
    (held,) = small(finish_kernel, [near(held.shape)], early, *rest_over_z(keep, came))
    return states, jnp.transpose(held, (1, 0, 2))[None]


def solution(mesh):
    return jax.shard_map(
        shards,
        mesh=mesh,
        in_specs=(
            P("blk", None, None, None),
            P("blk", "rows", None, None),
            P(None, "blk", "rows", None, None),
            P("blk", "rows", None, None),
            P(None, "rows", None, None),
        ),
        out_specs=(P(None, "blk", "rows", None, None), P("blk", "rows", None, None)),
        check_vma=False,
    )
```

```python
import functools

import jax
import jax.numpy as jnp
from jax import lax
from jax.experimental import pallas as pl
from jax.experimental.pallas import tpu as pltpu
from jax.sharding import PartitionSpec as P

TICKS = 3
BF = jnp.bfloat16
F32 = jnp.float32
VMEM_BYTES = 12 * 1024 * 1024
SMALL_VMEM_BYTES = 6 * 1024 * 1024


def whole(memory=pltpu.VMEM):
    return pl.BlockSpec(memory_space=memory)


def fill_shifted(shift_ref, rows):
    for index, row in enumerate(rows):
        columns = row.shape[1]
        place = lax.broadcasted_iota(jnp.int32, row.shape, 1)
        nothing = jnp.zeros_like(row)
        shift_ref[0, index] = jnp.where(place == columns - 1, nothing, pltpu.roll(row, columns - 1, 1))
        shift_ref[1, index] = row
        shift_ref[2, index] = jnp.where(place == 0, nothing, pltpu.roll(row, 1, 1))


def near(shape, kind=BF):
    return jax.ShapeDtypeStruct(shape, kind)


def kept(value):
    return pltpu.with_memory_space_constraint(value, pltpu.HBM)


def fetch(pairs, sems):
    copies = [pltpu.make_async_copy(source, target, sems.at[i]) for i, (source, target) in enumerate(pairs)]
    for copy in copies:
        copy.start()
    return copies


def gradient_rows(edges, image):
    if image is None:
        up, top, mid, bot, down = edges
        return [up[...], top[...], *[mid[i] for i in range(mid.shape[0])], bot[...], down[...]]
    return [edges[0][...], *[image[i] for i in range(image.shape[0])], edges[1][...]]


def back_kernel(tick, *refs):
    refs = list(refs)
    first, last = tick == 0, tick == TICKS - 1
    restart = lax.axis_index("blk") == lax.axis_size("blk") - tick - 1
    edges = [refs.pop(0) for _ in range(2 if first else 5)]
    image_far = refs.pop(0) if first else None
    kernel = refs.pop(0)
    pieces = [refs.pop(0) for _ in range(2)] if tick == 1 else []
    saved_far = refs.pop(0)
    fresh_far = None if last else refs.pop(0)
    if not first:
        refs.pop(0)
    states = refs.pop(0)
    outs = [] if last else [refs.pop(0) for _ in range(3)]
    joined = kernel if last else refs.pop(0)
    shift_ref, turned, result, saved = [refs.pop(0) for _ in range(4)]
    fresh = None if last else refs.pop(0)
    image = refs.pop(0) if first else None
    sems, sem = refs
    height, channels, _ = saved.shape
    pairs = [(saved_far.at[tick, 0], saved)]
    if first:
        pairs = [(image_far.at[0], image), (kernel, joined)] + pairs
    if not last:
        pairs.append((fresh_far.at[tick], fresh))
    copies = fetch(pairs, sems)
    if first:
        copies.pop(0).wait()
    fill_shifted(shift_ref, gradient_rows(edges, image))
    if first:
        copies.pop(0).wait()
    for k, piece in enumerate(pieces):
        part = piece.shape[1]
        start = pl.multiple_of(lax.rem(lax.axis_index("rows") // 4 + k, 2) * part, part)
        joined[:, pl.ds(start, part), :] = kernel[:, pl.ds(start, part), :] + piece[...]
    for b in range(3):
        for j in range(3):
            turned[b, :, j * channels : (j + 1) * channels] = joined[3 * (2 - j) + b].T
    for copy in copies:
        copy.wait()
    copies = []
    for r in range(height):
        total = None
        for b in range(3):
            window = shift_ref[b, r : r + 3].reshape(3 * channels, -1)
            part = jnp.dot(turned[b], window, preferred_element_type=F32)
            total = part if total is None else total + part
        value = jnp.where(saved[r] > 0, total, 0.0).astype(BF)
        result[r] = value
        copy = pltpu.make_async_copy(result.at[r], states.at[tick, 0, r], sem.at[r])
        copy.start()
        copies.append(copy)
        if not last:
            value = jnp.where(restart, fresh[r], value)
            if r == 0:
                outs[0][...] = value
            elif r == height - 1:
                outs[2][...] = value
            else:
                outs[1][r - 1] = value
    for copy in copies:
        copy.wait()


def back_project(tick, edges, image, kernel, pieces, saved, states, fresh):
    first, last = tick == 0, tick == TICKS - 1
    _, _, height, channels, columns = saved.shape
    args, specs = [], []

    def give(value, memory=pltpu.VMEM):
        args.append(kept(value) if memory is pl.ANY else value)
        specs.append(whole(memory))

    for value in edges:
        give(value)
    if first:
        give(image, pl.ANY)
        give(kernel, pl.ANY)
    else:
        for value in (kernel, *pieces):
            give(value)
    give(saved, pl.ANY)
    if not last:
        give(fresh, pl.ANY)
    alias = {}
    if not first:
        alias = {len(args): 0}
        give(states, pl.ANY)
    shapes = [jax.ShapeDtypeStruct((TICKS, 1, height, channels, columns), BF)]
    block = (height, channels, columns)
    scratch = [
        pltpu.VMEM((3, height + 2, channels, columns), BF),
        pltpu.VMEM((3, channels, 3 * channels), BF),
        pltpu.VMEM(block, BF),
        pltpu.VMEM(block, BF),
    ]
    if not last:
        shapes += [near((channels, columns)), near((height - 2, channels, columns)), near((channels, columns))]
        scratch.append(pltpu.VMEM(block, BF))
    if first:
        scratch.append(pltpu.VMEM(block, BF))
    if tick == 1:
        shapes.append(near(kernel.shape))
    if first:
        scratch = [pltpu.VMEM(kernel.shape, BF)] + scratch
    scratch += [pltpu.SemaphoreType.DMA((4,)), pltpu.SemaphoreType.DMA((height,))]
    return pl.pallas_call(
        functools.partial(back_kernel, tick),
        out_shape=shapes,
        in_specs=specs,
        out_specs=[whole(pl.ANY)] + [whole()] * (len(shapes) - 1),
        scratch_shapes=scratch,
        input_output_aliases=alias,
        compiler_params=pltpu.CompilerParams(vmem_limit_bytes=VMEM_BYTES),
        cost_estimate=pl.CostEstimate(flops=1, bytes_accessed=1, transcendentals=0),
        name="back",
    )(*args)


def weight_kernel(tick, scale, *refs):
    refs = list(refs)
    first = tick == 0
    edges = [refs.pop(0) for _ in range(2 if first else 5)]
    image_far = refs.pop(0) if first else None
    saved_far = refs.pop(0)
    out = refs.pop(0)
    sems = refs.pop()
    image = refs.pop() if first else None
    saved = refs.pop()
    shift_ref = refs.pop()
    height, channels, _ = saved.shape
    pairs = [(saved_far.at[tick, 0], saved)]
    if first:
        pairs.insert(0, (image_far.at[0], image))
    copies = fetch(pairs, sems)
    if first:
        copies.pop(0).wait()
    fill_shifted(shift_ref, gradient_rows(edges, image))
    copies.pop(0).wait()
    inputs = [jnp.maximum(saved[r], 0) for r in range(height)]
    part = channels // 4
    piece = part // 4
    for k in range(4):
        total = None
        for r in range(height):
            left = shift_ref[:, r : r + 3, k * part : (k + 1) * part, :].reshape(9 * part, -1)
            term = lax.dot_general(left, inputs[r], (((1,), (1,)), ((), ())), preferred_element_type=F32)
            total = term if total is None else total + term
        total = total * scale
        for b in range(3):
            for j in range(3):
                base = (3 * b + j) * part
                tap = 3 * (2 - j) + b
                for q in range(4):
                    value = total[base + q * piece : base + (q + 1) * piece]
                    out[k, q, tap] = value.astype(BF)


def weight_terms(tick, edges, image, saved, scale):
    _, _, height, channels, columns = saved.shape
    rest = [(edge, pltpu.VMEM) for edge in edges]
    if tick == 0:
        rest.append((kept(image), pl.ANY))
    rest.append((kept(saved), pl.ANY))
    block = pltpu.VMEM((height, channels, columns), BF)
    return pl.pallas_call(
        functools.partial(weight_kernel, tick, scale),
        out_shape=near((4, 4, 9, channels // 16, channels)),
        in_specs=[whole(memory) for _, memory in rest],
        out_specs=whole(),
        scratch_shapes=[pltpu.VMEM((3, height + 2, channels, columns), BF)]
        + [block] * (2 if tick == 0 else 1)
        + [pltpu.SemaphoreType.DMA((2,))],
        compiler_params=pltpu.CompilerParams(vmem_limit_bytes=VMEM_BYTES),
        cost_estimate=pl.CostEstimate(flops=1, bytes_accessed=1, transcendentals=0),
        name="weight",
    )(*[value for value, _ in rest])


def opening_kernel(kernel, image, half, top, bot, sems):
    part = half.shape[1]
    start = pl.multiple_of(lax.rem(lax.axis_index("rows") // 4, 2) * part, part)
    last = image.shape[1] - 1
    pairs = [(image.at[0, 0], top), (image.at[0, last], bot), (kernel.at[:, pl.ds(start, part), :], half)]
    for copy in fetch(pairs, sems):
        copy.wait()


def opening(kernel, image):
    taps, rows, columns = kernel.shape
    edge = near(image.shape[2:])
    return pl.pallas_call(
        opening_kernel,
        out_shape=[near((taps, rows // 2, columns)), edge, edge],
        in_specs=[whole(pl.ANY)] * 2,
        out_specs=[whole()] * 3,
        scratch_shapes=[pltpu.SemaphoreType.DMA((3,))],
        compiler_params=pltpu.CompilerParams(vmem_limit_bytes=SMALL_VMEM_BYTES),
        cost_estimate=pl.CostEstimate(flops=1, bytes_accessed=1, transcendentals=0),
        name="opening",
    )(kept(kernel), kept(image))


def pair_kernel(zero, two, other, *outs):
    odd = lax.axis_index("blk") % 2 == 1
    for k in range(4):
        place = lax.rem(lax.axis_index("rows") // 4 + k, 4)
        for q in range(4):
            more = other[place, q].astype(F32)
            early = zero[place, q].astype(F32) + jnp.where(odd, more, 0.0)
            late = two[place, q].astype(F32) + jnp.where(odd, 0.0, more)
            outs[k][q] = early.astype(outs[k].dtype)
            outs[4 + k][q] = late.astype(outs[4 + k].dtype)


def regroup_kernel(own, one, two, three, keep, send):
    place = lax.rem(lax.axis_index("rows"), 4)
    beside = place + 1 - 2 * lax.rem(place, 2)
    spots = (place, lax.rem(place + 2, 4), beside, lax.rem(beside + 2, 4))
    for k, spot in enumerate(spots):
        value = (own[spot] + one[spot].astype(F32)) + (two[spot].astype(F32) + three[spot].astype(F32))
        if k < 2:
            keep[k] = value
        else:
            send[k - 2] = value.astype(BF)


def halve_kernel(keep, came, kept_on, send):
    kept_on[...] = keep[0] + came[0].astype(F32)
    send[...] = (keep[1] + came[1].astype(F32)).astype(BF)


def finish_kernel(held, keep, came, out):
    out[...] = (held[...].astype(F32) + (keep[...] + came[...].astype(F32))).astype(BF)


def small(kernel, shapes, *args):
    return pl.pallas_call(
        kernel,
        out_shape=shapes,
        in_specs=[whole()] * len(args),
        out_specs=[whole()] * len(shapes),
        compiler_params=pltpu.CompilerParams(vmem_limit_bytes=SMALL_VMEM_BYTES),
        cost_estimate=pl.CostEstimate(flops=1, bytes_accessed=1, transcendentals=0),
        name=kernel.__name__,
    )(*args)


def after(values, *others):
    return lax.optimization_barrier((values, others))[0]


def along(value, move):
    return lax.ppermute(value, "rows", [(x * 4 + z, move(x, z)) for x in range(4) for z in range(4)])


def along_odd(value, move):
    pairs = [(b * 16 + x * 4 + z, b * 16 + move(x, z)) for b in range(1, 16, 2) for x in range(4) for z in range(4)]
    return lax.ppermute(value, ("blk", "rows"), pairs)


def kernels_back(value, pairs):
    places = [(x * 4 + z, x * 4 + 3 - z, x * 4 + z) for x in range(4) for z in range(4)]
    moves = [(a * 16 + (far if a // 8 != b // 8 else here), b * 16 + there) for a, b in pairs for here, far, there in places]
    return lax.ppermute(value, ("blk", "rows"), moves)


def around(value, pairs):
    return lax.ppermute(value, "blk", pairs)


def with_edges(top, mid, bot):
    up = lax.ppermute(bot, "rows", [(i, i + 1) for i in range(15)])
    down = lax.ppermute(top, "rows", [(i + 1, i) for i in range(15)])
    return up, top, mid, bot, down


def over_x(parts):
    return [parts[0]] + [along(parts[k], lambda x, z, k=k: ((x + k) % 4) * 4 + z) for k in (1, 2, 3)]


def part_over_z(parts, held):
    shape = (2, *held.shape)
    keep, send = small(regroup_kernel, [near(shape, F32), near(shape)], *parts)
    return keep, along(send, lambda x, z: x * 4 + (z ^ 1))


def rest_over_z(keep, came):
    shape = keep.shape[1:]
    keep, send = small(halve_kernel, [near(shape, F32), near(shape)], keep, came)
    return keep, along(send, lambda x, z: x * 4 + (z ^ 2))


def shards(section_weights, grad_acc, saved_inputs, cotangent, fresh_grads):
    kernel = jnp.transpose(section_weights[0], (1, 0, 2))
    held = jnp.transpose(grad_acc[0], (1, 0, 2))
    height = cotangent.shape[1]
    columns = cotangent.shape[3]
    scale = float(16 * height * columns) ** (-0.5)
    back_by = lambda by: [(b, (b - by) % 16) for b in range(16)]
    evens = range(0, 16, 2)

    def back(tick, edges, kernel, pieces, states):
        return back_project(tick, edges, cotangent, kernel, pieces, saved_inputs, states, fresh_grads)

    def weight(tick, edges):
        return weight_terms(tick, edges, cotangent, saved_inputs, scale)

    half, top, bot = opening(kernel, cotangent)
    half = kernels_back(half, [(b, (b - 1) % 16) for b in evens])
    up, _, _, _, down = with_edges(top, None, bot)
    half, kernel_here = after((half, kernel), up, down)
    kernel_one = around(kernel_here, [(b + 1, b) for b in evens])
    states, *parts = back(0, (up, down), kernel, (), None)
    edges_one = with_edges(*parts)
    halves = [half, along_odd(half, lambda x, z: (x ^ 1) * 4 + z)]
    sums_zero = weight(0, after((up, down), parts[0]))
    edges_one = after(edges_one, sums_zero)
    states, *parts, used = back(1, edges_one, kernel_one, halves, states)
    edges_two = with_edges(*parts)
    sums_one = weight(1, after(edges_one, parts[0]))
    edges_two, used, sums_one = lax.optimization_barrier((edges_two, used, sums_one))
    other = around(sums_one, [(b, b ^ 1) for b in range(16)])
    kernel_two = kernels_back(used, back_by(1))
    sums_two = weight(2, edges_two)
    part = (4, *held.shape)
    spread = ([near(part, F32)] + [near(part)] * 3) * 2
    both = small(pair_kernel, spread, sums_zero, sums_two, other)
    first, last = over_x(both[:4]), over_x(both[4:])
    keep, came = part_over_z(first, held)
    (states,) = back(2, after(edges_two, keep), kernel_two, (), states)
    keep, came = rest_over_z(keep, after(came, states))
    last = after(last, came)
    (early,) = small(finish_kernel, [near(held.shape)], held, keep, came)
    early = around(early, back_by(2))
    keep, came = part_over_z(last, held)
    (held,) = small(finish_kernel, [near(held.shape)], early, *rest_over_z(keep, came))
    return states, jnp.transpose(held, (1, 0, 2))[None]


def solution(mesh):
    return jax.shard_map(
        shards,
        mesh=mesh,
        in_specs=(
            P("blk", None, None, None),
            P("blk", "rows", None, None),
            P(None, "blk", "rows", None, None),
            P("blk", "rows", None, None),
            P(None, "rows", None, None),
        ),
        out_specs=(P(None, "blk", "rows", None, None), P("blk", "rows", None, None)),
        check_vma=False,
    )
```

```python
import functools

import jax
import jax.numpy as jnp
from jax import lax
from jax.experimental import pallas as pl
from jax.experimental.pallas import tpu as pltpu
from jax.sharding import PartitionSpec as P

TICKS = 3
BF = jnp.bfloat16
F32 = jnp.float32
VMEM_BYTES = 12 * 1024 * 1024
SMALL_VMEM_BYTES = 6 * 1024 * 1024


def whole(memory=pltpu.VMEM):
    return pl.BlockSpec(memory_space=memory)


def fill_shifted(shift_ref, rows):
    for index, row in enumerate(rows):
        columns = row.shape[1]
        place = lax.broadcasted_iota(jnp.int32, row.shape, 1)
        nothing = jnp.zeros_like(row)
        shift_ref[0, index] = jnp.where(place == columns - 1, nothing, pltpu.roll(row, columns - 1, 1))
        shift_ref[1, index] = row
        shift_ref[2, index] = jnp.where(place == 0, nothing, pltpu.roll(row, 1, 1))


def near(shape, kind=BF):
    return jax.ShapeDtypeStruct(shape, kind)


def kept(value):
    return pltpu.with_memory_space_constraint(value, pltpu.HBM)


def fetch(pairs, sems):
    copies = [pltpu.make_async_copy(source, target, sems.at[i]) for i, (source, target) in enumerate(pairs)]
    for copy in copies:
        copy.start()
    return copies


def gradient_rows(edges, image):
    if image is None:
        up, top, mid, bot, down = edges
        return [up[...], top[...], *[mid[i] for i in range(mid.shape[0])], bot[...], down[...]]
    return [edges[0][...], *[image[i] for i in range(image.shape[0])], edges[1][...]]


def back_kernel(tick, *refs):
    refs = list(refs)
    first, last = tick == 0, tick == TICKS - 1
    restart = lax.axis_index("blk") == lax.axis_size("blk") - tick - 1
    edges = [refs.pop(0) for _ in range(2 if first else 5)]
    image_far = refs.pop(0) if first else None
    kernel = refs.pop(0)
    pieces = [refs.pop(0) for _ in range(2)] if tick == 1 else []
    saved_far = refs.pop(0)
    fresh_far = None if last else refs.pop(0)
    if not first:
        refs.pop(0)
    states = refs.pop(0)
    outs = [] if last else [refs.pop(0) for _ in range(3)]
    joined = kernel if last else refs.pop(0)
    shift_ref, turned, result, saved = [refs.pop(0) for _ in range(4)]
    fresh = None if last else refs.pop(0)
    image = refs.pop(0) if first else None
    sems, sem = refs
    height, channels, _ = saved.shape
    pairs = [(saved_far.at[tick, 0], saved)]
    if first:
        pairs = [(image_far.at[0], image), (kernel, joined)] + pairs
    if not last:
        pairs.append((fresh_far.at[tick], fresh))
    copies = fetch(pairs, sems)
    if first:
        copies.pop(0).wait()
    fill_shifted(shift_ref, gradient_rows(edges, image))
    if first:
        copies.pop(0).wait()
    for k, piece in enumerate(pieces):
        part = piece.shape[1]
        start = pl.multiple_of(lax.rem(lax.axis_index("rows") // 4 + k, 2) * part, part)
        joined[:, pl.ds(start, part), :] = kernel[:, pl.ds(start, part), :] + piece[...]
    for b in range(3):
        for j in range(3):
            turned[b, :, j * channels : (j + 1) * channels] = joined[3 * (2 - j) + b].T
    for copy in copies:
        copy.wait()
    copies = []
    for r in range(height):
        total = None
        for b in range(3):
            window = shift_ref[b, r : r + 3].reshape(3 * channels, -1)
            part = jnp.dot(turned[b], window, preferred_element_type=F32)
            total = part if total is None else total + part
        value = jnp.where(saved[r] > 0, total, 0.0).astype(BF)
        result[r] = value
        copy = pltpu.make_async_copy(result.at[r], states.at[tick, 0, r], sem.at[r])
        copy.start()
        copies.append(copy)
        if not last:
            value = jnp.where(restart, fresh[r], value)
            if r == 0:
                outs[0][...] = value
            elif r == height - 1:
                outs[2][...] = value
            else:
                outs[1][r - 1] = value
    for copy in copies:
        copy.wait()


def back_project(tick, edges, image, kernel, pieces, saved, states, fresh):
    first, last = tick == 0, tick == TICKS - 1
    _, _, height, channels, columns = saved.shape
    args, specs = [], []

    def give(value, memory=pltpu.VMEM):
        args.append(kept(value) if memory is pl.ANY else value)
        specs.append(whole(memory))

    for value in edges:
        give(value)
    if first:
        give(image, pl.ANY)
        give(kernel, pl.ANY)
    else:
        for value in (kernel, *pieces):
            give(value)
    give(saved, pl.ANY)
    if not last:
        give(fresh, pl.ANY)
    alias = {}
    if not first:
        alias = {len(args): 0}
        give(states, pl.ANY)
    shapes = [jax.ShapeDtypeStruct((TICKS, 1, height, channels, columns), BF)]
    block = (height, channels, columns)
    scratch = [
        pltpu.VMEM((3, height + 2, channels, columns), BF),
        pltpu.VMEM((3, channels, 3 * channels), BF),
        pltpu.VMEM(block, BF),
        pltpu.VMEM(block, BF),
    ]
    if not last:
        shapes += [near((channels, columns)), near((height - 2, channels, columns)), near((channels, columns))]
        scratch.append(pltpu.VMEM(block, BF))
    if first:
        scratch.append(pltpu.VMEM(block, BF))
    if tick == 1:
        shapes.append(near(kernel.shape))
    if first:
        scratch = [pltpu.VMEM(kernel.shape, BF)] + scratch
    scratch += [pltpu.SemaphoreType.DMA((4,)), pltpu.SemaphoreType.DMA((height,))]
    return pl.pallas_call(
        functools.partial(back_kernel, tick),
        out_shape=shapes,
        in_specs=specs,
        out_specs=[whole(pl.ANY)] + [whole()] * (len(shapes) - 1),
        scratch_shapes=scratch,
        input_output_aliases=alias,
        compiler_params=pltpu.CompilerParams(vmem_limit_bytes=VMEM_BYTES),
        cost_estimate=pl.CostEstimate(flops=1, bytes_accessed=1, transcendentals=0),
        name="back",
    )(*args)


def weight_kernel(tick, scale, *refs):
    refs = list(refs)
    first = tick == 0
    edges = [refs.pop(0) for _ in range(2 if first else 5)]
    image_far = refs.pop(0) if first else None
    saved_far = refs.pop(0)
    out = refs.pop(0)
    sems = refs.pop()
    image = refs.pop() if first else None
    saved = refs.pop()
    shift_ref = refs.pop()
    height, channels, _ = saved.shape
    pairs = [(saved_far.at[tick, 0], saved)]
    if first:
        pairs.insert(0, (image_far.at[0], image))
    copies = fetch(pairs, sems)
    if first:
        copies.pop(0).wait()
    fill_shifted(shift_ref, gradient_rows(edges, image))
    copies.pop(0).wait()
    inputs = [jnp.maximum(saved[r], 0) for r in range(height)]
    part = channels // 4
    piece = part // 4
    for k in range(4):
        total = None
        for r in range(height):
            left = shift_ref[:, r : r + 3, k * part : (k + 1) * part, :].reshape(9 * part, -1)
            term = lax.dot_general(left, inputs[r], (((1,), (1,)), ((), ())), preferred_element_type=F32)
            total = term if total is None else total + term
        total = total * scale
        for b in range(3):
            for j in range(3):
                base = (3 * b + j) * part
                tap = 3 * (2 - j) + b
                for q in range(4):
                    value = total[base + q * piece : base + (q + 1) * piece]
                    out[k, q, tap] = value.astype(BF)


def weight_terms(tick, edges, image, saved, scale):
    _, _, height, channels, columns = saved.shape
    rest = [(edge, pltpu.VMEM) for edge in edges]
    if tick == 0:
        rest.append((kept(image), pl.ANY))
    rest.append((kept(saved), pl.ANY))
    block = pltpu.VMEM((height, channels, columns), BF)
    return pl.pallas_call(
        functools.partial(weight_kernel, tick, scale),
        out_shape=near((4, 4, 9, channels // 16, channels)),
        in_specs=[whole(memory) for _, memory in rest],
        out_specs=whole(),
        scratch_shapes=[pltpu.VMEM((3, height + 2, channels, columns), BF)]
        + [block] * (2 if tick == 0 else 1)
        + [pltpu.SemaphoreType.DMA((2,))],
        compiler_params=pltpu.CompilerParams(vmem_limit_bytes=VMEM_BYTES),
        cost_estimate=pl.CostEstimate(flops=1, bytes_accessed=1, transcendentals=0),
        name="weight",
    )(*[value for value, _ in rest])


def opening_kernel(kernel, image, half, top, bot, sems):
    part = half.shape[1]
    start = pl.multiple_of(lax.rem(lax.axis_index("rows") // 4, 2) * part, part)
    last = image.shape[1] - 1
    pairs = [(image.at[0, 0], top), (image.at[0, last], bot), (kernel.at[:, pl.ds(start, part), :], half)]
    for copy in fetch(pairs, sems):
        copy.wait()


def opening(kernel, image):
    taps, rows, columns = kernel.shape
    edge = near(image.shape[2:])
    return pl.pallas_call(
        opening_kernel,
        out_shape=[near((taps, rows // 2, columns)), edge, edge],
        in_specs=[whole(pl.ANY)] * 2,
        out_specs=[whole()] * 3,
        scratch_shapes=[pltpu.SemaphoreType.DMA((3,))],
        compiler_params=pltpu.CompilerParams(vmem_limit_bytes=SMALL_VMEM_BYTES),
        cost_estimate=pl.CostEstimate(flops=1, bytes_accessed=1, transcendentals=0),
        name="opening",
    )(kept(kernel), kept(image))


def pair_kernel(zero, two, other, *outs):
    odd = lax.axis_index("blk") % 2 == 1
    for k in range(4):
        place = lax.rem(lax.axis_index("rows") // 4 + k, 4)
        for q in range(4):
            more = other[place, q].astype(F32)
            early = zero[place, q].astype(F32) + jnp.where(odd, more, 0.0)
            late = two[place, q].astype(F32) + jnp.where(odd, 0.0, more)
            outs[k][q] = early.astype(outs[k].dtype)
            outs[4 + k][q] = late.astype(outs[4 + k].dtype)


def regroup_kernel(own, one, two, three, keep, send):
    place = lax.rem(lax.axis_index("rows"), 4)
    beside = place + 1 - 2 * lax.rem(place, 2)
    spots = (place, lax.rem(place + 2, 4), beside, lax.rem(beside + 2, 4))
    for k, spot in enumerate(spots):
        value = (own[spot] + one[spot].astype(F32)) + (two[spot].astype(F32) + three[spot].astype(F32))
        if k < 2:
            keep[k] = value
        else:
            send[k - 2] = value.astype(BF)


def halve_kernel(keep, came, kept_on, send):
    kept_on[...] = keep[0] + came[0].astype(F32)
    send[...] = (keep[1] + came[1].astype(F32)).astype(BF)


def finish_kernel(held, keep, came, out):
    out[...] = (held[...].astype(F32) + (keep[...] + came[...].astype(F32))).astype(BF)


def small(kernel, shapes, *args):
    return pl.pallas_call(
        kernel,
        out_shape=shapes,
        in_specs=[whole()] * len(args),
        out_specs=[whole()] * len(shapes),
        compiler_params=pltpu.CompilerParams(vmem_limit_bytes=SMALL_VMEM_BYTES),
        cost_estimate=pl.CostEstimate(flops=1, bytes_accessed=1, transcendentals=0),
        name=kernel.__name__,
    )(*args)


def after(values, *others):
    return lax.optimization_barrier((values, others))[0]


def along(value, move):
    return lax.ppermute(value, "rows", [(x * 4 + z, move(x, z)) for x in range(4) for z in range(4)])


def along_odd(value, move):
    pairs = [(b * 16 + x * 4 + z, b * 16 + move(x, z)) for b in range(1, 16, 2) for x in range(4) for z in range(4)]
    return lax.ppermute(value, ("blk", "rows"), pairs)


def kernels_back(value, pairs):
    places = [(x * 4 + z, x * 4 + 3 - z, x * 4 + z) for x in range(4) for z in range(4)]
    moves = [(a * 16 + (far if a // 8 != b // 8 else here), b * 16 + there) for a, b in pairs for here, far, there in places]
    return lax.ppermute(value, ("blk", "rows"), moves)


def around(value, pairs):
    return lax.ppermute(value, "blk", pairs)


def with_edges(top, mid, bot):
    up = lax.ppermute(bot, "rows", [(i, i + 1) for i in range(15)])
    down = lax.ppermute(top, "rows", [(i + 1, i) for i in range(15)])
    return up, top, mid, bot, down


def over_x(parts):
    return [parts[0]] + [along(parts[k], lambda x, z, k=k: ((x + k) % 4) * 4 + z) for k in (1, 2, 3)]


def part_over_z(parts, held):
    shape = (2, *held.shape)
    keep, send = small(regroup_kernel, [near(shape, F32), near(shape)], *parts)
    return keep, along(send, lambda x, z: x * 4 + (z ^ 1))


def rest_over_z(keep, came):
    shape = keep.shape[1:]
    keep, send = small(halve_kernel, [near(shape, F32), near(shape)], keep, came)
    return keep, along(send, lambda x, z: x * 4 + (z ^ 2))


def shards(section_weights, grad_acc, saved_inputs, cotangent, fresh_grads):
    kernel = jnp.transpose(section_weights[0], (1, 0, 2))
    held = jnp.transpose(grad_acc[0], (1, 0, 2))
    height = cotangent.shape[1]
    columns = cotangent.shape[3]
    scale = float(16 * height * columns) ** (-0.5)
    back_by = lambda by: [(b, (b - by) % 16) for b in range(16)]
    evens = range(0, 16, 2)

    def back(tick, edges, kernel, pieces, states):
        return back_project(tick, edges, cotangent, kernel, pieces, saved_inputs, states, fresh_grads)

    def weight(tick, edges):
        return weight_terms(tick, edges, cotangent, saved_inputs, scale)

    half, top, bot = opening(kernel, cotangent)
    half = kernels_back(half, [(b, (b - 1) % 16) for b in evens])
    up, _, _, _, down = with_edges(top, None, bot)
    half, kernel_here = after((half, kernel), up, down)
    kernel_one = around(kernel_here, [(b + 1, b) for b in evens])
    states, *parts = back(0, (up, down), kernel, (), None)
    edges_one = with_edges(*parts)
    halves = [half, along_odd(half, lambda x, z: (x ^ 1) * 4 + z)]
    sums_zero = weight(0, after((up, down), parts[0]))
    edges_one = after(edges_one, sums_zero)
    states, *parts, used = back(1, edges_one, kernel_one, halves, states)
    edges_two = with_edges(*parts)
    sums_one = weight(1, after(edges_one, parts[0]))
    edges_two, sums_one = lax.optimization_barrier((edges_two, sums_one))
    other = around(sums_one, [(b, b ^ 1) for b in range(16)])
    sums_two = weight(2, edges_two)
    part = (4, *held.shape)
    spread = ([near(part, F32)] + [near(part)] * 3) * 2
    both = small(pair_kernel, spread, sums_zero, sums_two, other)
    first, last = over_x(both[:4]), over_x(both[4:])
    kernel_two = kernels_back(after(used, both[0]), back_by(1))
    keep, came = rest_over_z(*part_over_z(first, held))
    last = after(last, came)
    (early,) = small(finish_kernel, [near(held.shape)], held, keep, came)
    early = around(early, back_by(2))
    keep, came = rest_over_z(*part_over_z(last, held))
    (states,) = back(2, after(edges_two, keep), kernel_two, (), states)
    early = after(early, states)
    (held,) = small(finish_kernel, [near(held.shape)], early, keep, came)
    return states, jnp.transpose(held, (1, 0, 2))[None]


def solution(mesh):
    return jax.shard_map(
        shards,
        mesh=mesh,
        in_specs=(
            P("blk", None, None, None),
            P("blk", "rows", None, None),
            P(None, "blk", "rows", None, None),
            P("blk", "rows", None, None),
            P(None, "rows", None, None),
        ),
        out_specs=(P(None, "blk", "rows", None, None), P("blk", "rows", None, None)),
        check_vma=False,
    )
```
